32 devices in a mesh: dp: 8 (over z, y), mp: 4 (over x, core).
Axes of the slice: x: 2, y: 2, z: 4, core: 2. Of those that a mesh axis runs over, the one named last changes fastest.
Arguments:
- hidden: bfloat16 [64, 32, 1024], P(('dp', 'mp')), may hold values from -96 to 96, as said below
- query_weight: bfloat16 [1024, 1024], P('dp', 'mp'), may hold values from -0.1875 to 0.1875
- w_key: bfloat16 [1024, 1024], P('dp', 'mp'), may hold values from -0.1875 to 0.1875
- w_value: bfloat16 [1024, 1024], P('dp', 'mp'), may hold values from -0.1875 to 0.1875
- rel_table: bfloat16 [512, 1024], P('dp'), may hold values from -6 to 6
- rel_bucket: int32 [32, 32], replicated, may hold values from 0 to 511
- w_out: bfloat16 [1024, 1024], P('mp', 'dp'), may hold values from -0.1875 to 0.1875
- w_up: bfloat16 [1024, 4096], P('dp', 'mp'), may hold values from -0.1875 to 0.1875
- w_down: bfloat16 [4096, 1024], P('mp', 'dp'), may hold values from -0.09375 to 0.09375
- w_proj: bfloat16 [1024, 128], P(('dp', 'mp')), may hold values from -0.1875 to 0.1875
- pages: bfloat16 [2048, 128, 128], P('dp'), may hold values from -0.59765625 to 0.59765625
- page_len: int32 [2048], P('dp'), may hold values from 1 to 128
- slot_per_page: int32 [2048], replicated, may hold values from 0 to 2047, as said below
- candidates: int32 [64, 16, 4], P(('dp', 'mp')), may hold values from 0 to 2047, as said below
Outputs:
- query_vectors: bfloat16 [64, 32, 128], P(('dp', 'mp'))
- scores: float32 [64, 16], P(('dp', 'mp'))
The draws below stay inside these ranges and needn't reach their ends.
Inputs may be any that keep to these rules, and one draw needn't show every extreme that they name: slot_per_page is a permutation of the slots; the page in slot s is held by index s // 256 of dp. `candidates`: among the 128 page ids of the 2 queries of one device (queries in aligned blocks of 2), at most 32 have slots held by any one index of dp, and in every such block some index of dp holds exactly 32 of them. `hidden`: token states are finite.
All inputs are finite; a program needn't handle non-finite values.
Results may differ from the reference program's by a relative error of at most 0.025.
Values may be sent and summed in bfloat16 or wider, within the bound.
A program may use at most 64 MiB of HBM per device.

```python
import jax
import jax.numpy as jnp
from jax import lax

D = 1024
HEADS = 16
FF = 4096
BUCKETS = 512
HD = 64
E = 128
QLEN = 32
PTOK = 128
PPC = 4
QRY_DEV = 2
NCAND = 16
PG_DEV = 256
QUERIES = 64
PAGES = 2048
HOLDERS = 8
REQ = 128
CAP = 32


def request_tables(key):
    perm = jax.random.permutation(jax.random.fold_in(key, 11), PAGES).astype(jnp.int32)
    inverse = jnp.argsort(perm).astype(jnp.int32)
    total = HOLDERS * CAP
    dest_of = jnp.arange(total, dtype=jnp.int32) // CAP
    hot = jax.random.permutation(jax.random.fold_in(key, 12), HOLDERS)[:2].astype(jnp.int32)
    is_hot = jnp.any(dest_of[:, None] == hot[None, :], axis=1)
    keys = jax.random.split(jax.random.fold_in(key, 13), QUERIES // QRY_DEV)

    def one_block(sub):
        first, second, third = jax.random.split(sub, 3)
        noise = jax.random.randint(first, (total,), 0, 1024, dtype=jnp.int32)
        rank = jnp.where(is_hot, 0, 1 + noise) * total + jnp.arange(total, dtype=jnp.int32)
        chosen = dest_of[jnp.argsort(rank)[:REQ]]
        chosen = chosen[jax.random.permutation(second, REQ)]
        local = jax.random.randint(third, (REQ,), 0, PG_DEV, dtype=jnp.int32)
        return inverse[chosen * PG_DEV + local]
    lists = jax.vmap(one_block)(keys).reshape(QUERIES, NCAND, PPC)
    return (perm, lists.astype(jnp.int32))


def draw_slot_per_page(key, part):
    return request_tables(key)[0]


def draw_candidates(key, part):
    return request_tables(key)[1]


def draw_hidden(key, part):
    first = jax.random.fold_in(jax.random.fold_in(key, 21), 0)
    value = jnp.clip(jax.random.normal(first, (QUERIES, QLEN, D), jnp.float32), -6.0, 6.0)
    return value.astype(jnp.bfloat16)


def plant(values, own_key, smallest, top_value):
    dims = values.shape
    place = [jax.random.randint(jax.random.fold_in(own_key, axis), (), 0, dims[axis]) for axis in range(len(dims))]
    values = values.at[tuple(place)].set(smallest)
    longest = dims.index(max(dims))
    place[longest] = (place[longest] + 1) % dims[longest]
    return values.at[tuple(place)].set(top_value)


def block_scale(own_key, extent, cuts, smallest, high):
    def one(position, parts):
        draws = jax.random.uniform(jax.random.fold_in(jax.random.fold_in(own_key, 6), position), (parts,), jnp.float32, smallest / len(cuts), high / len(cuts))
        return jnp.repeat(jnp.exp(draws), extent[position] // parts).reshape((-1,) + (1,) * (len(extent) - position - 1))

    level = one(*cuts[0])
    for cut in cuts[1:]:
        level = level * one(*cut)
    return level


def centred(key, shape, spread, bound, shards=(), held_as=jnp.bfloat16):
    array = spread * jax.random.normal(key, shape, jnp.float32)
    if shards:
        array = array * block_scale(key, shape, shards, -0.22, 0.18)
    return jnp.clip(array, -bound, bound).astype(held_as)


def setup_inputs(seed: int = 0) -> dict:
    seeds = jax.random.split(jax.random.key(seed), 15)
    return {
        "hidden": draw_hidden(jax.random.fold_in(seeds[14], 71), 0),
        "query_weight": centred(seeds[1], (D, D), D ** -0.5, 0.1875, ((0, 8), (1, 4))),
        "w_key": centred(seeds[2], (D, D), D ** -0.5, 0.1875, ((0, 8), (1, 4))),
        "w_value": centred(seeds[3], (D, D), D ** -0.5, 0.1875, ((0, 8), (1, 4))),
        "rel_table": centred(seeds[4], (BUCKETS, D), 1.0, 6.0, ((0, 8),)),
        "rel_bucket": plant(jax.random.randint(seeds[5], (QLEN, QLEN), 0, BUCKETS), jax.random.fold_in(seeds[5], 1), 0, BUCKETS - 1).astype(jnp.int32),
        "w_out": centred(seeds[6], (D, D), D ** -0.5, 0.1875, ((0, 4), (1, 8))),
        "w_up": centred(seeds[7], (D, FF), D ** -0.5, 0.1875, ((0, 8), (1, 4))),
        "w_down": centred(seeds[8], (FF, D), FF ** -0.5, 0.09375, ((0, 4), (1, 8))),
        "w_proj": centred(seeds[9], (D, E), D ** -0.5, 0.1875, ((0, 32),)),
        "pages": centred(seeds[10], (PAGES, PTOK, E), 0.09, 0.59765625, ((0, 8),)),
        "page_len": plant(jax.random.randint(seeds[11], (PAGES,), 1, PTOK + 1), jax.random.fold_in(seeds[11], 1), 1, PTOK).astype(jnp.int32),
        "slot_per_page": draw_slot_per_page(jax.random.fold_in(seeds[14], 71), 0),
        "candidates": draw_candidates(jax.random.fold_in(seeds[14], 71), 0),
    }


def layer_norm(value):
    mean = lax.optimization_barrier(jnp.mean(value, axis=-1, keepdims=True))
    centered = value - mean
    var = lax.optimization_barrier(jnp.mean(centered * centered, axis=-1, keepdims=True))
    return centered / jnp.sqrt(var + 1e-07)

def reference(hidden, query_weight, w_key, w_value, rel_table, rel_bucket, w_out, w_up, w_down, w_proj, pages, page_len, slot_per_page, candidates):
    flat = hidden.reshape(QUERIES * QLEN, D)
    qx = jnp.dot(flat, query_weight, preferred_element_type=jnp.float32).astype(jnp.bfloat16)
    kx = jnp.dot(flat, w_key, preferred_element_type=jnp.float32).astype(jnp.bfloat16)
    vx = jnp.dot(flat, w_value, preferred_element_type=jnp.float32).astype(jnp.bfloat16)
    qr = jnp.dot(rel_table, query_weight, preferred_element_type=jnp.float32).astype(jnp.bfloat16)
    kr = jnp.dot(rel_table, w_key, preferred_element_type=jnp.float32).astype(jnp.bfloat16)
    qx = qx.reshape(QUERIES, QLEN, HEADS, HD)
    kx = kx.reshape(QUERIES, QLEN, HEADS, HD)
    vx = vx.reshape(QUERIES, QLEN, HEADS, HD)
    qr32 = qr.reshape(BUCKETS, HEADS, HD).astype(jnp.float32)
    key_relative_single = kr.reshape(BUCKETS, HEADS, HD).astype(jnp.float32)
    rows = jnp.arange(QLEN, dtype=jnp.int32)[:, None]
    scale = 1.0 / jnp.sqrt(jnp.float32(3 * HD))

    def attend(block):
        qone, kone, vone = block
        query_single_float = qone.astype(jnp.float32)
        k32 = kone.astype(jnp.float32)
        content = jnp.einsum('ihd,jhd->hij', query_single_float, k32)
        along_axis_name = jnp.einsum('xwe,ywe->wxy', query_single_float, key_relative_single)
        c2p = along_axis_name[:, rows, rel_bucket]
        back = jnp.einsum('jhd,bhd->hjb', k32, qr32)
        p2c = jnp.swapaxes(back[:, rows, rel_bucket], 1, 2)
        logits = (content + c2p + p2c) * scale
        probs = jax.nn.softmax(logits, axis=-1).astype(jnp.bfloat16)
        context_rows = jnp.einsum('hij,jhd->ihd', probs.astype(jnp.float32), vone.astype(jnp.float32))
        return context_rows.astype(jnp.bfloat16).reshape(QLEN, D)
    context_rows = lax.map(attend, (qx, kx, vx)).reshape(QUERIES * QLEN, D)
    attn = jnp.dot(context_rows, w_out, preferred_element_type=jnp.float32)
    mid = layer_norm(flat.astype(jnp.float32) + attn).astype(jnp.bfloat16)
    inner = jax.nn.gelu(jnp.dot(mid, w_up, preferred_element_type=jnp.float32), approximate=False).astype(jnp.bfloat16)
    mlp = jnp.dot(inner, w_down, preferred_element_type=jnp.float32)
    state = layer_norm(mid.astype(jnp.float32) + mlp).astype(jnp.bfloat16)
    proj = jnp.dot(state, w_proj, preferred_element_type=jnp.float32)
    vectors = (proj / jnp.sqrt(lax.optimization_barrier(jnp.sum(proj * proj, axis=-1, keepdims=True)) + 1e-06)).astype(jnp.bfloat16)
    vectors = vectors.reshape(QUERIES, QLEN, E)
    token_positions = jnp.arange(PTOK, dtype=jnp.int32)

    def score(block):
        vec, cand = block
        slots = slot_per_page[cand]
        chosen = pages[slots].astype(jnp.float32)
        lens = page_len[slots]
        sim = jnp.einsum('ie,cpte->cpit', vec.astype(jnp.float32), chosen)
        valid = token_positions[None, None, None, :] < lens[:, :, None, None]
        best = lax.optimization_barrier(jnp.max(jnp.where(valid, sim, -1e+30), axis=-1))
        return lax.optimization_barrier(jnp.sum(lax.optimization_barrier(jnp.max(best, axis=1)), axis=-1))
    scores = lax.map(score, (vectors, candidates))
    return (vectors, scores)
```

```python
import functools

import jax
import jax.numpy as jnp
from jax import lax
from jax.experimental import pallas as pl
from jax.experimental.pallas import tpu as pltpu
from jax.sharding import PartitionSpec as P

HD = 64
MESH = pl.DeviceIdType.MESH


def layer_norm(value):
    mean = jnp.mean(value, axis=-1, keepdims=True)
    centered = value - mean
    var = jnp.mean(centered * centered, axis=-1, keepdims=True)
    return centered / jnp.sqrt(var + 1e-07)


def add_rows(left, piece):
    return jnp.dot(left, piece, preferred_element_type=jnp.float32)


def gather_kernel(n, nm, count, *refs):
    hid, wp = refs[:2]
    ins = refs[2 : 2 + count]
    hid_out, wp_out = refs[2 + count : 4 + count]
    outs = refs[4 + count : 4 + 2 * count]
    wp_own, local_sem, mp_send, mp_recv, send_sem, recv_sem = refs[4 + 2 * count :]
    dp, mp = lax.axis_index("dp"), lax.axis_index("mp")
    half = n // 2
    row, col = dp // 2, dp % 2
    pos = row + col * (n - 1 - 2 * row)

    def at(p):
        p = (p + 2 * n) % n
        h = p // half
        return 2 * (p + h * (n - 1 - 2 * p)) + h

    right, left = at(pos + 1), at(pos - 1)
    barrier = pltpu.get_barrier_semaphore()
    for d in (left, right):
        pl.semaphore_signal(barrier, inc=1, device_id=(d, mp), device_id_type=MESH)
    for k in range(1, nm):
        pl.semaphore_signal(
            barrier, inc=1, device_id=(dp, (mp + k) % nm), device_id_type=MESH
        )
    pl.semaphore_wait(barrier, 2 + nm - 1)

    local = [pltpu.make_async_copy(wp, wp_own.at[mp], local_sem.at[0])]
    local.append(pltpu.make_async_copy(hid, hid_out.at[mp], local_sem.at[1]))
    for i in range(count):
        local.append(pltpu.make_async_copy(ins[i], outs[i].at[dp], local_sem.at[2 + i]))
    mp_copies = []
    for which, (src, dst) in enumerate(((wp, wp_own), (hid, hid_out))):
        for k in range(1, nm):
            copy = pltpu.make_async_remote_copy(
                src_ref=src,
                dst_ref=dst.at[mp],
                send_sem=mp_send.at[which, k - 1],
                recv_sem=mp_recv.at[which, k - 1],
                device_id=(dp, (mp + k) % nm),
                device_id_type=MESH,
            )
            copy.start()
            mp_copies.append(copy)

    all_outs = list(outs) + [wp_out]
    pending = {}

    def send(step, i, way):
        owner = at(pos - step) if way == 0 else at(pos + step)
        if i == count:
            h = nm // 2
            cut = pl.ds(way * h, h)
            src = wp_own.at[cut] if step == 0 else wp_out.at[owner, cut]
            dst = wp_out.at[owner, cut]
        else:
            src = ins[i].at[way] if step == 0 else outs[i].at[owner, way]
            dst = outs[i].at[owner, way]
        copy = pltpu.make_async_remote_copy(
            src_ref=src,
            dst_ref=dst,
            send_sem=send_sem.at[step, i, way],
            recv_sem=recv_sem.at[step, i, way],
            device_id=(right if way == 0 else left, mp),
            device_id_type=MESH,
        )
        copy.start()
        pending[step, i, way] = copy

    for step in range(n - 1):
        for i in range(count + 1):
            if step == 0 and i == count:
                for c in local:
                    c.start()
                local[0].wait()
                for c in mp_copies[: nm - 1]:
                    c.wait_recv()
                own = pltpu.make_async_copy(wp_own, wp_out.at[dp], local_sem.at[0])
                own.start()
            for way in range(2):
                if step:
                    pending[step - 1, i, way].wait_recv()
                send(step, i, way)
    for (step, i, way), copy in pending.items():
        if step == n - 2:
            copy.wait_recv()
    for c in mp_copies[nm - 1 :]:
        c.wait_recv()
    own.wait()
    for c in local[1:]:
        c.wait()
    for c in mp_copies:
        c.wait_send()
    for copy in pending.values():
        copy.wait_send()


def gather_all(n, nm, hidden, w_proj, arrays):
    arrays = [a.reshape((2, a.shape[0] // 2) + a.shape[1:]) for a in arrays]
    count = len(arrays)
    bf = jnp.bfloat16
    shapes = [
        jax.ShapeDtypeStruct((nm,) + hidden.shape, bf),
        jax.ShapeDtypeStruct((n, nm) + w_proj.shape, bf),
    ] + [jax.ShapeDtypeStruct((n,) + a.shape, bf) for a in arrays]
    out = pl.pallas_call(
        functools.partial(gather_kernel, n, nm, count),
        out_shape=shapes,
        in_specs=[pl.BlockSpec(memory_space=pl.ANY)] * (count + 2),
        out_specs=[pl.BlockSpec(memory_space=pl.ANY)] * (count + 2),
        scratch_shapes=[
            pltpu.VMEM((nm,) + w_proj.shape, bf),
            pltpu.SemaphoreType.DMA((count + 2,)),
            pltpu.SemaphoreType.DMA((2, nm - 1)),
            pltpu.SemaphoreType.DMA((2, nm - 1)),
            pltpu.SemaphoreType.DMA((n - 1, count + 1, 2)),
            pltpu.SemaphoreType.DMA((n - 1, count + 1, 2)),
        ],
        compiler_params=pltpu.CompilerParams(collective_id=0, has_side_effects=True),
    )(hidden, w_proj, *arrays)
    flat = [o.reshape((n, o.shape[1] * o.shape[2]) + o.shape[3:]) for o in out[2:]]
    return out[0], out[1], flat


def score_kernel(n, cap, rows, where_ref, lens_ref, vec_ref, pages_ref, out_ref, buf, sems):
    ptok = buf.shape[2]
    group = 8

    def page_copy(s, r):
        return pltpu.make_async_copy(
            pages_ref.at[where_ref[s * cap + r]], buf.at[s, r], sems.at[s]
        )

    def start(s, carry):
        for r in range(cap):
            page_copy(s, r).start()
        return carry

    lax.fori_loop(0, n, start, 0)
    token = lax.broadcasted_iota(jnp.int32, (ptok, rows), 0)

    def work(s, carry):
        pltpu.make_async_copy(buf.at[s], buf.at[s], sems.at[s]).wait()
        vec = vec_ref[s]
        for g in range(cap // group):
            chunk = buf[s, pl.ds(g * group, group)].reshape(group * ptok, -1)
            sim = lax.dot_general(
                chunk, vec, (((1,), (1,)), ((), ())), preferred_element_type=jnp.float32
            )
            best = []
            for r in range(group):
                length = lens_ref[where_ref[s * cap + g * group + r]]
                part = sim[r * ptok : (r + 1) * ptok]
                part = jnp.where(token < length, part, -1e30)
                best.append(jnp.max(part, axis=0, keepdims=True))
            out_ref[s, pl.ds(g * group, group)] = jnp.concatenate(best, axis=0)
        return carry

    lax.fori_loop(0, n, work, 0)


def score_pages(where, lens, vecs, pages):
    n, cap = where.shape
    rows = vecs.shape[1]
    grid_spec = pltpu.PrefetchScalarGridSpec(
        num_scalar_prefetch=2,
        grid=(1,),
        in_specs=[
            pl.BlockSpec(vecs.shape, lambda i, a, b: (0, 0, 0)),
            pl.BlockSpec(memory_space=pl.ANY),
        ],
        out_specs=pl.BlockSpec((n, cap, rows), lambda i, a, b: (0, 0, 0)),
        scratch_shapes=[
            pltpu.VMEM((n, cap) + pages.shape[1:], pages.dtype),
            pltpu.SemaphoreType.DMA((n,)),
        ],
    )
    return pl.pallas_call(
        functools.partial(score_kernel, n, cap, rows),
        grid_spec=grid_spec,
        out_shape=jax.ShapeDtypeStruct((n, cap, rows), jnp.float32),
        compiler_params=pltpu.CompilerParams(vmem_limit_bytes=40 * 2**20),
    )(where.reshape(-1), lens, vecs, pages)


def body(
    hidden,
    query_weight,
    w_key,
    w_value,
    rel_table,
    rel_bucket,
    w_out,
    w_up,
    w_down,
    w_proj,
    pages,
    page_len,
    slot_per_page,
    candidates,
):
    n, nm = lax.axis_size("dp"), lax.axis_size("mp")
    qry_dev, qlen, width = hidden.shape
    heads_local = query_weight.shape[1] // HD
    cols = query_weight.shape[1]

    pg_dev = pages.shape[0]
    ncand, ppc = (candidates.shape[1], candidates.shape[2])
    req = qry_dev * ncand * ppc
    cap = 2 * req // n
    slots = slot_per_page[candidates.reshape(req)]
    dest = slots // pg_dev
    order = jnp.arange(req, dtype=jnp.int32)
    earlier = (dest[:, None] == dest[None, :]) & (order[None, :] < order[:, None])
    place = jnp.sum(earlier.astype(jnp.int32), axis=1)
    index = dest * cap + place
    codes = jnp.zeros((n * cap,), jnp.int32).at[index].set(slots % pg_dev)
    where_local = lax.all_to_all(
        codes.reshape(n, cap), "dp", split_axis=0, concat_axis=0, tiled=True
    )

    tokens, proj_w, (wq, wk, wv, rel, wo, wu, wd) = gather_all(
        n,
        nm,
        hidden.reshape(qry_dev * qlen, width),
        w_proj,
        (query_weight, w_key, w_value, rel_table, w_out, w_up, w_down),
    )
    group = nm * qry_dev
    flat = tokens.reshape(group * qlen, width)
    wq, wk, wv = (w.reshape(width, cols) for w in (wq, wk, wv))
    rel = rel.reshape(-1, width)
    wo = jnp.transpose(wo, (1, 0, 2)).reshape(wo.shape[1], width)
    wd = jnp.transpose(wd, (1, 0, 2)).reshape(wd.shape[1], width)
    wu = wu.reshape(width, -1)
    qsum = add_rows(flat, wq)
    ksum = add_rows(flat, wk)
    vsum = add_rows(flat, wv)
    rel_q = add_rows(rel, wq).astype(jnp.bfloat16)
    rel_k = add_rows(rel, wk).astype(jnp.bfloat16)
    nbuck = rel_q.shape[0]
    qx = qsum.astype(jnp.bfloat16).reshape(group, qlen, heads_local, HD)
    kx = ksum.astype(jnp.bfloat16).reshape(group, qlen, heads_local, HD)
    vx = vsum.astype(jnp.bfloat16).reshape(group, qlen, heads_local, HD)
    rel_q = rel_q.reshape(nbuck, heads_local, HD)
    rel_k = rel_k.reshape(nbuck, heads_local, HD)
    onehot = (rel_bucket[:, :, None] == jnp.arange(nbuck, dtype=jnp.int32)[None, None, :]).astype(
        jnp.float32
    )
    scale = 1.0 / jnp.sqrt(jnp.float32(3 * HD))
    content = jnp.einsum("qihd,qjhd->qhij", qx, kx, preferred_element_type=jnp.float32)
    along_axis_name = jnp.einsum("qihd,bhd->qhib", qx, rel_k, preferred_element_type=jnp.float32)
    c2p = jnp.einsum("qhib,ijb->qhij", along_axis_name, onehot, precision=lax.Precision.HIGHEST)
    back = jnp.einsum("qjhd,bhd->qhjb", kx, rel_q, preferred_element_type=jnp.float32)
    p2c = jnp.einsum("qhjb,jib->qhij", back, onehot, precision=lax.Precision.HIGHEST)
    logits = (content + c2p + p2c) * scale
    probs = jax.nn.softmax(logits, axis=-1).astype(jnp.bfloat16)
    context_rows = jnp.einsum("qhij,qjhd->qihd", probs, vx, preferred_element_type=jnp.float32)
    context_rows = context_rows.astype(jnp.bfloat16).reshape(group * qlen, cols)
    attn_terms = add_rows(context_rows, wo)
    attn = lax.psum_scatter(
        attn_terms.astype(jnp.bfloat16), "mp", scatter_dimension=0, tiled=True
    ).astype(jnp.float32)
    own = hidden.reshape(qry_dev * qlen, width).astype(jnp.float32)
    mid = layer_norm(own + attn).astype(jnp.bfloat16)
    mid_all = lax.all_gather(mid, "mp", axis=0, tiled=True)
    up = add_rows(mid_all, wu)
    inner = jax.nn.gelu(up, approximate=False).astype(jnp.bfloat16)
    down_terms = add_rows(inner, wd)
    mlp = lax.psum_scatter(
        down_terms.astype(jnp.bfloat16), "mp", scatter_dimension=0, tiled=True
    ).astype(jnp.float32)
    state = layer_norm(mid.astype(jnp.float32) + mlp).astype(jnp.bfloat16)
    width_out = w_proj.shape[1]
    proj = add_rows(state, proj_w.reshape(width, width_out))
    vectors = (proj / jnp.sqrt(jnp.sum(proj * proj, axis=-1, keepdims=True) + 1e-06)).astype(
        jnp.bfloat16
    )
    spread = jnp.broadcast_to(vectors[None], (n,) + vectors.shape)
    seen = lax.all_to_all(spread, "dp", split_axis=0, concat_axis=0, tiled=True)
    best = score_pages(where_local, page_len, seen, pages).astype(jnp.bfloat16)
    back_home = lax.all_to_all(best, "dp", split_axis=0, concat_axis=0, tiled=True)
    best = back_home.reshape(n * cap, qry_dev * qlen)[index].astype(jnp.float32)
    best = best.reshape(qry_dev, ncand, ppc, qry_dev, qlen)
    best = jnp.stack([best[q, :, :, q] for q in range(qry_dev)])
    scores = jnp.sum(jnp.max(best, axis=2), axis=-1)
    return (vectors.reshape(qry_dev, qlen, width_out), scores)


def solution(mesh):
    in_specs = (
        P(("dp", "mp"), None, None),
        P("dp", "mp"),
        P("dp", "mp"),
        P("dp", "mp"),
        P("dp", None),
        P(),
        P("mp", "dp"),
        P("dp", "mp"),
        P("mp", "dp"),
        P(("dp", "mp"), None),
        P("dp", None, None),
        P("dp"),
        P(),
        P(("dp", "mp"), None, None),
    )
    out_specs = (P(("dp", "mp"), None, None), P(("dp", "mp"), None))
    return jax.shard_map(body, mesh=mesh, in_specs=in_specs, out_specs=out_specs, check_vma=False)
```

```python
import functools

import jax
import jax.numpy as jnp
from jax import lax
from jax.experimental import pallas as pl
from jax.experimental.pallas import tpu as pltpu
from jax.sharding import PartitionSpec as P

HD = 64
MESH = pl.DeviceIdType.MESH


def layer_norm(value):
    mean = jnp.mean(value, axis=-1, keepdims=True)
    centered = value - mean
    var = jnp.mean(centered * centered, axis=-1, keepdims=True)
    return centered / jnp.sqrt(var + 1e-07)


def add_rows(left, piece):
    return jnp.dot(left, piece, preferred_element_type=jnp.float32)


def gather_kernel(n, nm, count, *refs):
    hid, wp, codes = refs[:3]
    ins = refs[3 : 3 + count]
    hid_out, wp_out, codes_out = refs[3 + count : 6 + count]
    outs = refs[6 + count : 6 + 2 * count]
    wp_own, local_sem, mp_send, mp_recv, code_send, code_recv, send_sem, recv_sem = refs[
        6 + 2 * count :
    ]
    dp, mp = lax.axis_index("dp"), lax.axis_index("mp")
    half = n // 2
    row, col = dp // 2, dp % 2
    pos = row + col * (n - 1 - 2 * row)

    def at(p):
        p = (p + 2 * n) % n
        h = p // half
        return 2 * (p + h * (n - 1 - 2 * p)) + h

    right, left = at(pos + 1), at(pos - 1)
    barrier = pltpu.get_barrier_semaphore()
    for k in range(1, n):
        pl.semaphore_signal(
            barrier, inc=1, device_id=((dp + k) % n, mp), device_id_type=MESH
        )
    for k in range(1, nm):
        pl.semaphore_signal(
            barrier, inc=1, device_id=(dp, (mp + k) % nm), device_id_type=MESH
        )
    pl.semaphore_wait(barrier, n - 1 + nm - 1)

    local = [pltpu.make_async_copy(wp, wp_own.at[mp], local_sem.at[0])]
    local.append(pltpu.make_async_copy(hid, hid_out.at[mp], local_sem.at[1]))
    for i in range(count):
        local.append(pltpu.make_async_copy(ins[i], outs[i].at[dp], local_sem.at[2 + i]))
    mp_copies = []
    for which, (src, dst) in enumerate(((wp, wp_own), (hid, hid_out))):
        for k in range(1, nm):
            copy = pltpu.make_async_remote_copy(
                src_ref=src,
                dst_ref=dst.at[mp],
                send_sem=mp_send.at[which, k - 1],
                recv_sem=mp_recv.at[which, k - 1],
                device_id=(dp, (mp + k) % nm),
                device_id_type=MESH,
            )
            copy.start()
            mp_copies.append(copy)

    local.append(pltpu.make_async_copy(codes.at[dp], codes_out.at[dp], local_sem.at[2 + count]))
    code_copies = []
    for k in range(1, n):
        copy = pltpu.make_async_remote_copy(
            src_ref=codes.at[(dp + k) % n],
            dst_ref=codes_out.at[dp],
            send_sem=code_send.at[k - 1],
            recv_sem=code_recv.at[k - 1],
            device_id=((dp + k) % n, mp),
            device_id_type=MESH,
        )
        copy.start()
        code_copies.append(copy)
    pending = {}

    def send(step, i, way):
        owner = at(pos - step) if way == 0 else at(pos + step)
        if i == count:
            h = nm // 2
            cut = pl.ds(way * h, h)
            src = wp_own.at[cut] if step == 0 else wp_out.at[owner, cut]
            dst = wp_out.at[owner, cut]
        else:
            src = ins[i].at[way] if step == 0 else outs[i].at[owner, way]
            dst = outs[i].at[owner, way]
        copy = pltpu.make_async_remote_copy(
            src_ref=src,
            dst_ref=dst,
            send_sem=send_sem.at[step, i, way],
            recv_sem=recv_sem.at[step, i, way],
            device_id=(right if way == 0 else left, mp),
            device_id_type=MESH,
        )
        copy.start()
        pending[step, i, way] = copy

    for step in range(n - 1):
        for i in range(count + 1):
            if step == 0 and i == count:
                for c in local:
                    c.start()
                local[0].wait()
                for c in mp_copies[: nm - 1]:
                    c.wait_recv()
                own = pltpu.make_async_copy(wp_own, wp_out.at[dp], local_sem.at[0])
                own.start()
            for way in range(2):
                if step:
                    pending[step - 1, i, way].wait_recv()
                send(step, i, way)
    for (step, i, way), copy in pending.items():
        if step == n - 2:
            copy.wait_recv()
    for c in mp_copies[nm - 1 :]:
        c.wait_recv()
    for c in code_copies:
        c.wait()
    own.wait()
    for c in local[1:]:
        c.wait()
    for c in mp_copies:
        c.wait_send()
    for copy in pending.values():
        copy.wait_send()


def gather_all(n, nm, hidden, w_proj, codes, arrays):
    arrays = [a.reshape((2, a.shape[0] // 2) + a.shape[1:]) for a in arrays]
    count = len(arrays)
    bf = jnp.bfloat16
    shapes = [
        jax.ShapeDtypeStruct((nm,) + hidden.shape, bf),
        jax.ShapeDtypeStruct((n, nm) + w_proj.shape, bf),
        jax.ShapeDtypeStruct(codes.shape, jnp.int32),
    ] + [jax.ShapeDtypeStruct((n,) + a.shape, bf) for a in arrays]
    out = pl.pallas_call(
        functools.partial(gather_kernel, n, nm, count),
        out_shape=shapes,
        in_specs=[pl.BlockSpec(memory_space=pl.ANY)] * (count + 3),
        out_specs=[pl.BlockSpec(memory_space=pl.ANY)] * (count + 3),
        scratch_shapes=[
            pltpu.VMEM((nm,) + w_proj.shape, bf),
            pltpu.SemaphoreType.DMA((count + 3,)),
            pltpu.SemaphoreType.DMA((2, nm - 1)),
            pltpu.SemaphoreType.DMA((2, nm - 1)),
            pltpu.SemaphoreType.DMA((n - 1,)),
            pltpu.SemaphoreType.DMA((n - 1,)),
            pltpu.SemaphoreType.DMA((n - 1, count + 1, 2)),
            pltpu.SemaphoreType.DMA((n - 1, count + 1, 2)),
        ],
        compiler_params=pltpu.CompilerParams(collective_id=0, has_side_effects=True),
    )(hidden, w_proj, codes, *arrays)
    flat = [o.reshape((n, o.shape[1] * o.shape[2]) + o.shape[3:]) for o in out[3:]]
    return out[0], out[1], out[2], flat


def layer_kernel(n, nm, *refs):
    (ctx, hid, wo_in, wu_in, wd_in, wp_in, pages_in, where, lens, vec_out, back_out) = refs[:11]
    (wo, wu, wd, wp, pages, load_sem, send_a, recv_a, mid_all, send_d, recv_d) = refs[11:22]
    (seen, found, back, sem_s, sem_r, vec_s, vec_r, back_s, back_r) = refs[22:]
    dp, mp = lax.axis_index("dp"), lax.axis_index("mp")
    rows, width = hid.shape
    cap, ptok = back.shape[1], pages.shape[1]
    block = wo.shape[2]
    step_cols = max(256, block)
    per = step_cols // block
    chunks = width // step_cols
    loads = [
        pltpu.make_async_copy(src, dst, load_sem.at[i])
        for i, (src, dst) in enumerate(
            ((wo_in, wo), (wu_in, wu), (wd_in, wd), (wp_in, wp), (pages_in, pages))
        )
    ]
    for c in loads:
        c.start()
    barrier = pltpu.get_barrier_semaphore()
    for k in range(1, n):
        pl.semaphore_signal(
            barrier, inc=1, device_id=((dp + k) % n, mp), device_id_type=MESH
        )
    for k in range(1, nm):
        pl.semaphore_signal(
            barrier, inc=1, device_id=(dp, (mp + k) % nm), device_id_type=MESH
        )
    pl.semaphore_wait(barrier, n - 1 + nm - 1)

    def piece(w, j):
        parts = [w[j * per + t] for t in range(per)]
        return parts[0] if per == 1 else jnp.concatenate(parts, axis=1)

    def mp_copy(stage, k, j, src, dst):
        return pltpu.make_async_remote_copy(
            src_ref=src,
            dst_ref=dst,
            send_sem=sem_s.at[stage, k - 1, j],
            recv_sem=sem_r.at[stage, k - 1, j],
            device_id=(dp, (mp + k) % nm),
            device_id_type=MESH,
        )

    order = [k for k in range(1, nm) if k != 1] + [1]
    started = []

    loads[0].wait()
    own = []
    for j in range(chunks):
        weight = piece(wo, j)
        for k in order:
            block_rows = ctx[pl.ds(pl.multiple_of((mp + k) % nm * rows, rows), rows), :]
            send_a[k - 1, j] = add_rows(block_rows, weight).astype(jnp.bfloat16)
            copy = mp_copy(0, k, j, send_a.at[k - 1, j], recv_a.at[k - 1, j])
            copy.start()
            started.append(copy)
        own.append(add_rows(ctx[pl.ds(pl.multiple_of(mp * rows, rows), rows), :], weight))
    sums = []
    for j in range(chunks):
        total = own[j]
        for k in range(1, nm):
            mp_copy(0, k, j, send_a.at[k - 1, j], recv_a.at[k - 1, j]).wait_recv()
            total = total + recv_a[k - 1, j].astype(jnp.float32)
        sums.append(total)
    attn = jnp.concatenate(sums, axis=1)
    mid = layer_norm(hid[...].astype(jnp.float32) + attn).astype(jnp.bfloat16)
    mid_all[mp] = mid
    for k in order:
        copy = mp_copy(1, k, 0, mid_all.at[mp], mid_all.at[mp])
        copy.start()
        started.append(copy)
    loads[1].wait()
    loads[2].wait()
    for k in range(1, nm):
        mp_copy(1, k, 0, mid_all.at[mp], mid_all.at[mp]).wait_recv()
    group_mid = mid_all[...].reshape(nm * rows, width)
    inner = []
    hidden_cols = wu.shape[1]
    for j in range(hidden_cols // 256):
        up = add_rows(group_mid, wu[:, j * 256 : (j + 1) * 256])
        act = 0.5 * up * (1.0 + lax.erf(up * (0.5**0.5)))
        inner.append(act.astype(jnp.bfloat16))
    inner = jnp.concatenate(inner, axis=1)
    for j in range(chunks):
        down = add_rows(inner, piece(wd, j)).astype(jnp.bfloat16)
        send_d[j] = down.reshape(nm, rows, step_cols)
        for k in order:
            copy = mp_copy(2, k, j, send_d.at[j, (mp + k) % nm], recv_d.at[k - 1, j])
            copy.start()
            started.append(copy)
    sums = []
    for j in range(chunks):
        total = send_d[j, mp].astype(jnp.float32)
        for k in range(1, nm):
            mp_copy(2, k, j, send_d.at[j, mp], recv_d.at[k - 1, j]).wait_recv()
            total = total + recv_d[k - 1, j].astype(jnp.float32)
        sums.append(total)
    mlp = jnp.concatenate(sums, axis=1)
    state = layer_norm(mid_all[mp].astype(jnp.float32) + mlp).astype(jnp.bfloat16)
    loads[3].wait()
    proj = add_rows(state, wp[...])
    norm = jnp.sqrt(jnp.sum(proj * proj, axis=-1, keepdims=True) + 1e-06)
    vectors = (proj / norm).astype(jnp.bfloat16)
    vec_out[...] = vectors
    seen[dp] = vectors

    def vec_copy(k):
        return pltpu.make_async_remote_copy(
            src_ref=seen.at[dp],
            dst_ref=seen.at[dp],
            send_sem=vec_s.at[k - 1],
            recv_sem=vec_r.at[k - 1],
            device_id=((dp + k) % n, mp),
            device_id_type=MESH,
        )

    def back_copy(k):
        return pltpu.make_async_remote_copy(
            src_ref=found.at[k - 1],
            dst_ref=back.at[dp],
            send_sem=back_s.at[k - 1],
            recv_sem=back_r.at[k - 1],
            device_id=((dp - k + n) % n, mp),
            device_id_type=MESH,
        )

    for k in range(1, n):
        vec_copy(k).start()
    loads[4].wait()
    token = lax.broadcasted_iota(jnp.int32, (ptok, rows), 0)

    def match(source):
        vec = seen[source]
        best = []
        for g in range(0, cap, 8):
            slots = [where[source * cap + g + r] for r in range(8)]
            chunk = jnp.concatenate([pages[slot] for slot in slots], axis=0)
            sim = lax.dot_general(
                chunk, vec, (((1,), (1,)), ((), ())), preferred_element_type=jnp.float32
            )
            for r in range(8):
                part = sim[r * ptok : (r + 1) * ptok]
                part = jnp.where(token < lens[slots[r]], part, -1e30)
                best.append(jnp.max(part, axis=0, keepdims=True))
        return jnp.concatenate(best, axis=0).astype(jnp.bfloat16)

    back[dp] = match(dp)

    def work(k, carry):
        vec_copy(k).wait_recv()
        found[k - 1] = match((dp - k + n) % n)
        back_copy(k).start()
        return carry

    lax.fori_loop(1, n, work, 0)
    for k in range(1, n):
        back_copy(k).wait_recv()
    back_out[...] = back[...]
    for k in range(1, n):
        vec_copy(k).wait_send()
        back_copy(k).wait_send()
    for c in started:
        c.wait_send()


def layer_and_score(n, nm, cap, ctx, hid, wo, wu, wd, wp, pages, where, lens):
    rows, width = hid.shape
    block = wo.shape[2]
    step_cols = max(256, block)
    chunks = width // step_cols
    bf = jnp.bfloat16
    vmem = pl.BlockSpec(memory_space=pltpu.VMEM)
    smem = pl.BlockSpec(memory_space=pltpu.SMEM)
    far = pl.BlockSpec(memory_space=pl.ANY)
    dma = pltpu.SemaphoreType.DMA
    scratch = [pltpu.VMEM(a.shape, a.dtype) for a in (wo, wu, wd, wp, pages)] + [
        dma((5,)),
        pltpu.VMEM((nm - 1, chunks, rows, step_cols), bf),
        pltpu.VMEM((nm - 1, chunks, rows, step_cols), bf),
        pltpu.VMEM((nm, rows, width), bf),
        pltpu.VMEM((chunks, nm, rows, step_cols), bf),
        pltpu.VMEM((nm - 1, chunks, rows, step_cols), bf),
        pltpu.VMEM((n, rows, wp.shape[1]), bf),
        pltpu.VMEM((n - 1, cap, rows), bf),
        pltpu.VMEM((n, cap, rows), bf),
        dma((3, nm - 1, chunks)),
        dma((3, nm - 1, chunks)),
        dma((n - 1,)),
        dma((n - 1,)),
        dma((n - 1,)),
        dma((n - 1,)),
    ]
    return pl.pallas_call(
        functools.partial(layer_kernel, n, nm),
        out_shape=[
            jax.ShapeDtypeStruct((rows, wp.shape[1]), bf),
            jax.ShapeDtypeStruct((n, cap, rows), bf),
        ],
        in_specs=[vmem, vmem, far, far, far, far, far, smem, smem],
        out_specs=[vmem, vmem],
        scratch_shapes=scratch,
        compiler_params=pltpu.CompilerParams(
            collective_id=1, has_side_effects=True, vmem_limit_bytes=40 * 2**20
        ),
    )(ctx, hid, wo, wu, wd, wp, pages, where, lens)


def body(
    hidden,
    query_weight,
    w_key,
    w_value,
    rel_table,
    rel_bucket,
    w_out,
    w_up,
    w_down,
    w_proj,
    pages,
    page_len,
    slot_per_page,
    candidates,
):
    n, nm = lax.axis_size("dp"), lax.axis_size("mp")
    qry_dev, qlen, width = hidden.shape
    heads_local = query_weight.shape[1] // HD
    cols = query_weight.shape[1]

    pg_dev = pages.shape[0]
    ncand, ppc = (candidates.shape[1], candidates.shape[2])
    req = qry_dev * ncand * ppc
    cap = 2 * req // n
    slots = slot_per_page[candidates.reshape(req)]
    dest = slots // pg_dev
    order = jnp.arange(req, dtype=jnp.int32)
    earlier = (dest[:, None] == dest[None, :]) & (order[None, :] < order[:, None])
    place = jnp.sum(earlier.astype(jnp.int32), axis=1)
    index = dest * cap + place
    codes = jnp.zeros((n * cap,), jnp.int32).at[index].set(slots % pg_dev)
    tokens, proj_w, where_local, (wq, wk, wv, rel, wo, wu, wd) = gather_all(
        n,
        nm,
        hidden.reshape(qry_dev * qlen, width),
        w_proj,
        codes.reshape(n, 1, cap),
        (query_weight, w_key, w_value, rel_table, w_out, w_up, w_down),
    )
    group = nm * qry_dev
    flat = tokens.reshape(group * qlen, width)
    wq, wk, wv = (w.reshape(width, cols) for w in (wq, wk, wv))
    rel = rel.reshape(-1, width)
    wu = wu.reshape(width, -1)
    qsum = add_rows(flat, wq)
    ksum = add_rows(flat, wk)
    vsum = add_rows(flat, wv)
    rel_q = add_rows(rel, wq).astype(jnp.bfloat16)
    rel_k = add_rows(rel, wk).astype(jnp.bfloat16)
    nbuck = rel_q.shape[0]
    qx = qsum.astype(jnp.bfloat16).reshape(group, qlen, heads_local, HD)
    kx = ksum.astype(jnp.bfloat16).reshape(group, qlen, heads_local, HD)
    vx = vsum.astype(jnp.bfloat16).reshape(group, qlen, heads_local, HD)
    rel_q = rel_q.reshape(nbuck, heads_local, HD)
    rel_k = rel_k.reshape(nbuck, heads_local, HD)
    onehot = (rel_bucket[:, :, None] == jnp.arange(nbuck, dtype=jnp.int32)[None, None, :]).astype(
        jnp.float32
    )
    scale = 1.0 / jnp.sqrt(jnp.float32(3 * HD))
    content = jnp.einsum("qihd,qjhd->qhij", qx, kx, preferred_element_type=jnp.float32)
    along_axis_name = jnp.einsum("qihd,bhd->qhib", qx, rel_k, preferred_element_type=jnp.float32)
    c2p = jnp.einsum("qhib,ijb->qhij", along_axis_name, onehot, precision=lax.Precision.HIGHEST)
    back = jnp.einsum("qjhd,bhd->qhjb", kx, rel_q, preferred_element_type=jnp.float32)
    p2c = jnp.einsum("qhjb,jib->qhij", back, onehot, precision=lax.Precision.HIGHEST)
    logits = (content + c2p + p2c) * scale
    probs = jax.nn.softmax(logits, axis=-1).astype(jnp.bfloat16)
    context_rows = jnp.einsum("qhij,qjhd->qihd", probs, vx, preferred_element_type=jnp.float32)
    context_rows = context_rows.astype(jnp.bfloat16).reshape(group * qlen, cols)
    width_out = w_proj.shape[1]
    vectors, back_home = layer_and_score(
        n,
        nm,
        cap,
        context_rows,
        hidden.reshape(qry_dev * qlen, width),
        wo,
        wu,
        wd,
        proj_w.reshape(width, width_out),
        pages,
        where_local.reshape(-1),
        page_len,
    )
    best = back_home.reshape(n * cap, qry_dev * qlen)[index].astype(jnp.float32)
    best = best.reshape(qry_dev, ncand, ppc, qry_dev, qlen)
    best = jnp.stack([best[q, :, :, q] for q in range(qry_dev)])
    scores = jnp.sum(jnp.max(best, axis=2), axis=-1)
    return (vectors.reshape(qry_dev, qlen, width_out), scores)


def solution(mesh):
    in_specs = (
        P(("dp", "mp"), None, None),
        P("dp", "mp"),
        P("dp", "mp"),
        P("dp", "mp"),
        P("dp", None),
        P(),
        P("mp", "dp"),
        P("dp", "mp"),
        P("mp", "dp"),
        P(("dp", "mp"), None),
        P("dp", None, None),
        P("dp"),
        P(),
        P(("dp", "mp"), None, None),
    )
    out_specs = (P(("dp", "mp"), None, None), P(("dp", "mp"), None))
    return jax.shard_map(body, mesh=mesh, in_specs=in_specs, out_specs=out_specs, check_vma=False)
```

```python
import functools

import jax
import jax.numpy as jnp
from jax import lax
from jax.experimental import pallas as pl
from jax.experimental.pallas import tpu as pltpu
from jax.sharding import PartitionSpec as P

HD = 64
MESH = pl.DeviceIdType.MESH


def layer_norm(value):
    mean = jnp.mean(value, axis=-1, keepdims=True)
    centered = value - mean
    var = jnp.mean(centered * centered, axis=-1, keepdims=True)
    return centered / jnp.sqrt(var + 1e-07)


def add_rows(left, piece):
    return jnp.dot(left, piece, preferred_element_type=jnp.float32)


def gather_kernel(n, nm, count, *refs):
    hid, wp, codes, rel = refs[:4]
    ins = refs[4 : 4 + count]
    hid_out, wp_out, codes_out, rel_out = refs[4 + count : 8 + count]
    outs = refs[8 + count : 8 + 2 * count]
    (
        local_sem,
        mp_send,
        mp_recv,
        code_send,
        code_recv,
        fwd_send,
        fwd_recv,
        send_sem,
        recv_sem,
    ) = refs[8 + 2 * count :]
    dp, mp = lax.axis_index("dp"), lax.axis_index("mp")
    half = n // 2
    row, col = dp // 2, dp % 2
    pos = row + col * (n - 1 - 2 * row)
    part = rel.shape[2] // nm
    share = pl.ds(pl.multiple_of(mp * part, part), part)

    def at(p):
        p = (p + 2 * n) % n
        h = p // half
        return 2 * (p + h * (n - 1 - 2 * p)) + h

    right, left = at(pos + 1), at(pos - 1)
    barrier = pltpu.get_barrier_semaphore()
    for k in range(1, n):
        pl.semaphore_signal(
            barrier, inc=1, device_id=((dp + k) % n, mp), device_id_type=MESH
        )
    for k in range(1, nm):
        pl.semaphore_signal(
            barrier, inc=1, device_id=(dp, (mp + k) % nm), device_id_type=MESH
        )
    pl.semaphore_wait(barrier, n - 1 + nm - 1)

    pending = {}
    forwards = []

    def send(step, i, way):
        owner = at(pos - step) if way == 0 else at(pos + step)
        if i == 0:
            dst = rel_out.at[owner, way, :, share]
            src = rel.at[way, :, share] if step == 0 else dst
        elif i == 1:
            dst = wp_out.at[owner, mp, way]
            src = wp.at[way] if step == 0 else dst
        else:
            dst = outs[i - 2].at[owner, way]
            src = ins[i - 2].at[way] if step == 0 else dst
        copy = pltpu.make_async_remote_copy(
            src_ref=src,
            dst_ref=dst,
            send_sem=send_sem.at[step, i, way],
            recv_sem=recv_sem.at[step, i, way],
            device_id=(right if way == 0 else left, mp),
            device_id_type=MESH,
        )
        copy.start()
        pending[step, i, way] = copy

    def forward(step, i, way):
        owner = at(pos - step) if way == 0 else at(pos + step)
        piece = rel_out.at[owner, way, :, share] if i == 0 else wp_out.at[owner, mp, way]
        for k in range(1, nm):
            copy = pltpu.make_async_remote_copy(
                src_ref=piece,
                dst_ref=piece,
                send_sem=fwd_send.at[step - 1, i, way, k - 1],
                recv_sem=fwd_recv.at[step - 1, i, way, k - 1],
                device_id=(dp, (mp + k) % nm),
                device_id_type=MESH,
            )
            copy.start()
            forwards.append(copy)

    local = [
        pltpu.make_async_copy(wp, wp_out.at[dp, mp], local_sem.at[0]),
        pltpu.make_async_copy(hid, hid_out.at[mp], local_sem.at[1]),
        pltpu.make_async_copy(codes.at[dp], codes_out.at[dp], local_sem.at[2]),
        pltpu.make_async_copy(rel, rel_out.at[dp], local_sem.at[3]),
    ]
    for i in range(count):
        local.append(pltpu.make_async_copy(ins[i], outs[i].at[dp], local_sem.at[4 + i]))
    others = []

    def start_others():
        for which, (src, dst) in enumerate(((wp, wp_out.at[dp, mp]), (hid, hid_out.at[mp]))):
            for k in range(1, nm):
                others.append(
                    pltpu.make_async_remote_copy(
                        src_ref=src,
                        dst_ref=dst,
                        send_sem=mp_send.at[which, k - 1],
                        recv_sem=mp_recv.at[which, k - 1],
                        device_id=(dp, (mp + k) % nm),
                        device_id_type=MESH,
                    )
                )
        for k in range(1, n):
            others.append(
                pltpu.make_async_remote_copy(
                    src_ref=codes.at[(dp + k) % n],
                    dst_ref=codes_out.at[dp],
                    send_sem=code_send.at[k - 1],
                    recv_sem=code_recv.at[k - 1],
                    device_id=((dp + k) % n, mp),
                    device_id_type=MESH,
                )
            )
        for c in others + local:
            c.start()

    for step in range(n - 1):
        for i in range(count + 2):
            for way in range(2):
                if step:
                    pending[step - 1, i, way].wait_recv()
                send(step, i, way)
                if step and i < 2:
                    forward(step, i, way)
        if step == 0:
            start_others()
    for i in range(count + 2):
        for way in range(2):
            pending[n - 2, i, way].wait_recv()
            if i < 2:
                forward(n - 1, i, way)
    for c in others:
        c.wait()
    for c in local:
        c.wait()
    for c in forwards:
        c.wait()
    for copy in pending.values():
        copy.wait_send()


def gather_all(n, nm, hidden, w_proj, codes, rel, arrays):
    def halves(a):
        return a.reshape((2, a.shape[0] // 2) + a.shape[1:])

    w_proj, rel = halves(w_proj), halves(rel)
    arrays = [halves(a) for a in arrays]
    count = len(arrays)
    bf = jnp.bfloat16
    dma = pltpu.SemaphoreType.DMA
    shapes = [
        jax.ShapeDtypeStruct((nm,) + hidden.shape, bf),
        jax.ShapeDtypeStruct((n, nm) + w_proj.shape, bf),
        jax.ShapeDtypeStruct(codes.shape, jnp.int32),
    ] + [jax.ShapeDtypeStruct((n,) + a.shape, bf) for a in [rel] + arrays]
    out = pl.pallas_call(
        functools.partial(gather_kernel, n, nm, count),
        out_shape=shapes,
        in_specs=[pl.BlockSpec(memory_space=pl.ANY)] * (count + 4),
        out_specs=[pl.BlockSpec(memory_space=pl.ANY)] * (count + 4),
        scratch_shapes=[
            dma((count + 4,)),
            dma((2, nm - 1)),
            dma((2, nm - 1)),
            dma((n - 1,)),
            dma((n - 1,)),
            dma((n - 1, 2, 2, nm - 1)),
            dma((n - 1, 2, 2, nm - 1)),
            dma((n - 1, count + 2, 2)),
            dma((n - 1, count + 2, 2)),
        ],
        compiler_params=pltpu.CompilerParams(collective_id=0, has_side_effects=True),
    )(hidden, w_proj, codes, rel, *arrays)
    flat = [o.reshape((n, o.shape[1] * o.shape[2]) + o.shape[3:]) for o in out[3:]]
    return out[0], out[1], out[2], flat


def layer_kernel(n, nm, *refs):
    (ctx, hid, wo_in, wu_in, wd_in, wp_in, pages_in, where, lens, vec_out, back_out) = refs[:11]
    (wo, wu, wd, wp, pages, load_sem, send_a, recv_a, mid_all, send_d, recv_d) = refs[11:22]
    (seen, found, back, sem_s, sem_r, vec_s, vec_r, back_s, back_r) = refs[22:]
    dp, mp = lax.axis_index("dp"), lax.axis_index("mp")
    rows, width = hid.shape
    cap, ptok = back.shape[1], pages.shape[1]
    block = wo.shape[2]
    step_cols = max(256, block)
    per = step_cols // block
    chunks = width // step_cols
    loads = [
        pltpu.make_async_copy(src, dst, load_sem.at[i])
        for i, (src, dst) in enumerate(
            ((wo_in, wo), (wu_in, wu), (wd_in, wd), (wp_in, wp), (pages_in, pages))
        )
    ]
    for c in loads:
        c.start()
    barrier = pltpu.get_barrier_semaphore()
    for k in range(1, n):
        pl.semaphore_signal(
            barrier, inc=1, device_id=((dp + k) % n, mp), device_id_type=MESH
        )
    for k in range(1, nm):
        pl.semaphore_signal(
            barrier, inc=1, device_id=(dp, (mp + k) % nm), device_id_type=MESH
        )
    pl.semaphore_wait(barrier, n - 1 + nm - 1)

    def piece(w, j):
        parts = [w[j * per + t] for t in range(per)]
        return parts[0] if per == 1 else jnp.concatenate(parts, axis=1)

    def mp_copy(stage, k, j, src, dst):
        return pltpu.make_async_remote_copy(
            src_ref=src,
            dst_ref=dst,
            send_sem=sem_s.at[stage, k - 1, j],
            recv_sem=sem_r.at[stage, k - 1, j],
            device_id=(dp, (mp + k) % nm),
            device_id_type=MESH,
        )

    order = [k for k in range(1, nm) if k != 1] + [1]
    started = []

    loads[0].wait()
    own = []
    for j in range(chunks):
        weight = piece(wo, j)
        for k in order:
            block_rows = ctx[pl.ds(pl.multiple_of((mp + k) % nm * rows, rows), rows), :]
            send_a[k - 1, j] = add_rows(block_rows, weight).astype(jnp.bfloat16)
            copy = mp_copy(0, k, j, send_a.at[k - 1, j], recv_a.at[k - 1, j])
            copy.start()
            started.append(copy)
        own.append(add_rows(ctx[pl.ds(pl.multiple_of(mp * rows, rows), rows), :], weight))
    sums = []
    for j in range(chunks):
        total = own[j]
        for k in range(1, nm):
            mp_copy(0, k, j, send_a.at[k - 1, j], recv_a.at[k - 1, j]).wait_recv()
            total = total + recv_a[k - 1, j].astype(jnp.float32)
        sums.append(total)
    attn = jnp.concatenate(sums, axis=1)
    mid = layer_norm(hid[...].astype(jnp.float32) + attn).astype(jnp.bfloat16)
    mid_all[mp] = mid
    for k in order:
        copy = mp_copy(1, k, 0, mid_all.at[mp], mid_all.at[mp])
        copy.start()
        started.append(copy)
    loads[1].wait()
    loads[2].wait()
    for k in range(1, nm):
        mp_copy(1, k, 0, mid_all.at[mp], mid_all.at[mp]).wait_recv()
    group_mid = mid_all[...].reshape(nm * rows, width)
    inner = []
    hidden_cols = wu.shape[1]
    for j in range(hidden_cols // 256):
        up = add_rows(group_mid, wu[:, j * 256 : (j + 1) * 256])
        act = 0.5 * up * (1.0 + lax.erf(up * (0.5**0.5)))
        inner.append(act.astype(jnp.bfloat16))
    inner = jnp.concatenate(inner, axis=1)
    for j in range(chunks):
        down = add_rows(inner, piece(wd, j)).astype(jnp.bfloat16)
        send_d[j] = down.reshape(nm, rows, step_cols)
        for k in order:
            copy = mp_copy(2, k, j, send_d.at[j, (mp + k) % nm], recv_d.at[k - 1, j])
            copy.start()
            started.append(copy)
    sums = []
    for j in range(chunks):
        total = send_d[j, mp].astype(jnp.float32)
        for k in range(1, nm):
            mp_copy(2, k, j, send_d.at[j, mp], recv_d.at[k - 1, j]).wait_recv()
            total = total + recv_d[k - 1, j].astype(jnp.float32)
        sums.append(total)
    mlp = jnp.concatenate(sums, axis=1)
    state = layer_norm(mid_all[mp].astype(jnp.float32) + mlp).astype(jnp.bfloat16)
    loads[3].wait()
    proj = add_rows(state, wp[...])
    norm = jnp.sqrt(jnp.sum(proj * proj, axis=-1, keepdims=True) + 1e-06)
    vectors = (proj / norm).astype(jnp.bfloat16)
    vec_out[...] = vectors
    seen[dp] = vectors

    def vec_copy(k):
        return pltpu.make_async_remote_copy(
            src_ref=seen.at[dp],
            dst_ref=seen.at[dp],
            send_sem=vec_s.at[k - 1],
            recv_sem=vec_r.at[k - 1],
            device_id=((dp + k) % n, mp),
            device_id_type=MESH,
        )

    def back_copy(k):
        return pltpu.make_async_remote_copy(
            src_ref=found.at[k - 1],
            dst_ref=back.at[dp],
            send_sem=back_s.at[k - 1],
            recv_sem=back_r.at[k - 1],
            device_id=((dp - k + n) % n, mp),
            device_id_type=MESH,
        )

    for k in range(1, n):
        vec_copy(k).start()
    loads[4].wait()
    token = lax.broadcasted_iota(jnp.int32, (ptok, rows), 0)

    def match(source):
        vec = seen[source]
        best = []
        for g in range(0, cap, 8):
            slots = [where[source * cap + g + r] for r in range(8)]
            chunk = jnp.concatenate([pages[slot] for slot in slots], axis=0)
            sim = lax.dot_general(
                chunk, vec, (((1,), (1,)), ((), ())), preferred_element_type=jnp.float32
            )
            for r in range(8):
                part = sim[r * ptok : (r + 1) * ptok]
                part = jnp.where(token < lens[slots[r]], part, -1e30)
                best.append(jnp.max(part, axis=0, keepdims=True))
        return jnp.concatenate(best, axis=0).astype(jnp.bfloat16)

    back[dp] = match(dp)

    def work(k, carry):
        vec_copy(k).wait_recv()
        found[k - 1] = match((dp - k + n) % n)
        back_copy(k).start()
        return carry

    lax.fori_loop(1, n, work, 0)
    for k in range(1, n):
        back_copy(k).wait_recv()
    back_out[...] = back[...]
    for k in range(1, n):
        vec_copy(k).wait_send()
        back_copy(k).wait_send()
    for c in started:
        c.wait_send()


def layer_and_score(n, nm, cap, ctx, hid, wo, wu, wd, wp, pages, where, lens):
    rows, width = hid.shape
    block = wo.shape[2]
    step_cols = max(256, block)
    chunks = width // step_cols
    bf = jnp.bfloat16
    vmem = pl.BlockSpec(memory_space=pltpu.VMEM)
    smem = pl.BlockSpec(memory_space=pltpu.SMEM)
    far = pl.BlockSpec(memory_space=pl.ANY)
    dma = pltpu.SemaphoreType.DMA
    scratch = [pltpu.VMEM(a.shape, a.dtype) for a in (wo, wu, wd, wp, pages)] + [
        dma((5,)),
        pltpu.VMEM((nm - 1, chunks, rows, step_cols), bf),
        pltpu.VMEM((nm - 1, chunks, rows, step_cols), bf),
        pltpu.VMEM((nm, rows, width), bf),
        pltpu.VMEM((chunks, nm, rows, step_cols), bf),
        pltpu.VMEM((nm - 1, chunks, rows, step_cols), bf),
        pltpu.VMEM((n, rows, wp.shape[1]), bf),
        pltpu.VMEM((n - 1, cap, rows), bf),
        pltpu.VMEM((n, cap, rows), bf),
        dma((3, nm - 1, chunks)),
        dma((3, nm - 1, chunks)),
        dma((n - 1,)),
        dma((n - 1,)),
        dma((n - 1,)),
        dma((n - 1,)),
    ]
    return pl.pallas_call(
        functools.partial(layer_kernel, n, nm),
        out_shape=[
            jax.ShapeDtypeStruct((rows, wp.shape[1]), bf),
            jax.ShapeDtypeStruct((n, cap, rows), bf),
        ],
        in_specs=[vmem, vmem, far, far, far, far, far, smem, smem],
        out_specs=[vmem, vmem],
        scratch_shapes=scratch,
        compiler_params=pltpu.CompilerParams(
            collective_id=1, has_side_effects=True, vmem_limit_bytes=60 * 2**20
        ),
    )(ctx, hid, wo, wu, wd, wp, pages, where, lens)


def body(
    hidden,
    query_weight,
    w_key,
    w_value,
    rel_table,
    rel_bucket,
    w_out,
    w_up,
    w_down,
    w_proj,
    pages,
    page_len,
    slot_per_page,
    candidates,
):
    n, nm = lax.axis_size("dp"), lax.axis_size("mp")
    qry_dev, qlen, width = hidden.shape
    heads_local = query_weight.shape[1] // HD
    cols = query_weight.shape[1]

    pg_dev = pages.shape[0]
    ncand, ppc = (candidates.shape[1], candidates.shape[2])
    req = qry_dev * ncand * ppc
    cap = 2 * req // n
    slots = slot_per_page[candidates.reshape(req)]
    dest = slots // pg_dev
    order = jnp.arange(req, dtype=jnp.int32)
    earlier = (dest[:, None] == dest[None, :]) & (order[None, :] < order[:, None])
    place = jnp.sum(earlier.astype(jnp.int32), axis=1)
    index = dest * cap + place
    codes = jnp.zeros((n * cap,), jnp.int32).at[index].set(slots % pg_dev)
    tokens, proj_w, where_local, (rel, wq, wk, wv, wo, wu, wd) = gather_all(
        n,
        nm,
        hidden.reshape(qry_dev * qlen, width),
        w_proj,
        codes.reshape(n, 1, cap),
        rel_table,
        (query_weight, w_key, w_value, w_out, w_up, w_down),
    )
    group = nm * qry_dev
    flat = tokens.reshape(group * qlen, width)
    wq, wk, wv = (w.reshape(width, cols) for w in (wq, wk, wv))
    rel = rel.reshape(-1, width)
    wu = wu.reshape(width, -1)
    qsum = add_rows(flat, wq)
    ksum = add_rows(flat, wk)
    vsum = add_rows(flat, wv)
    rel_q = add_rows(rel, wq).astype(jnp.bfloat16)
    rel_k = add_rows(rel, wk).astype(jnp.bfloat16)
    nbuck = rel_q.shape[0]
    qx = qsum.astype(jnp.bfloat16).reshape(group, qlen, heads_local, HD)
    kx = ksum.astype(jnp.bfloat16).reshape(group, qlen, heads_local, HD)
    vx = vsum.astype(jnp.bfloat16).reshape(group, qlen, heads_local, HD)
    rel_q = rel_q.reshape(nbuck, heads_local, HD)
    rel_k = rel_k.reshape(nbuck, heads_local, HD)
    onehot = (rel_bucket[:, :, None] == jnp.arange(nbuck, dtype=jnp.int32)[None, None, :]).astype(
        jnp.float32
    )
    scale = 1.0 / jnp.sqrt(jnp.float32(3 * HD))
    content = jnp.einsum("qihd,qjhd->qhij", qx, kx, preferred_element_type=jnp.float32)
    along_axis_name = jnp.einsum("qihd,bhd->qhib", qx, rel_k, preferred_element_type=jnp.float32)
    c2p = jnp.einsum("qhib,ijb->qhij", along_axis_name, onehot, precision=lax.Precision.HIGHEST)
    back = jnp.einsum("qjhd,bhd->qhjb", kx, rel_q, preferred_element_type=jnp.float32)
    p2c = jnp.einsum("qhjb,jib->qhij", back, onehot, precision=lax.Precision.HIGHEST)
    logits = (content + c2p + p2c) * scale
    probs = jax.nn.softmax(logits, axis=-1).astype(jnp.bfloat16)
    context_rows = jnp.einsum("qhij,qjhd->qihd", probs, vx, preferred_element_type=jnp.float32)
    context_rows = context_rows.astype(jnp.bfloat16).reshape(group * qlen, cols)
    width_out = w_proj.shape[1]
    vectors, back_home = layer_and_score(
        n,
        nm,
        cap,
        context_rows,
        hidden.reshape(qry_dev * qlen, width),
        wo,
        wu,
        wd,
        proj_w.reshape(width, width_out),
        pages,
        where_local.reshape(-1),
        page_len,
    )
    best = back_home.reshape(n * cap, qry_dev * qlen)[index].astype(jnp.float32)
    best = best.reshape(qry_dev, ncand, ppc, qry_dev, qlen)
    best = jnp.stack([best[q, :, :, q] for q in range(qry_dev)])
    scores = jnp.sum(jnp.max(best, axis=2), axis=-1)
    return (vectors.reshape(qry_dev, qlen, width_out), scores)


def solution(mesh):
    in_specs = (
        P(("dp", "mp"), None, None),
        P("dp", "mp"),
        P("dp", "mp"),
        P("dp", "mp"),
        P("dp", None),
        P(),
        P("mp", "dp"),
        P("dp", "mp"),
        P("mp", "dp"),
        P(("dp", "mp"), None),
        P("dp", None, None),
        P("dp"),
        P(),
        P(("dp", "mp"), None, None),
    )
    out_specs = (P(("dp", "mp"), None, None), P(("dp", "mp"), None))
    return jax.shard_map(body, mesh=mesh, in_specs=in_specs, out_specs=out_specs, check_vma=False)
```

```python
import functools

import jax
import jax.numpy as jnp
from jax import lax
from jax.experimental import pallas as pl
from jax.experimental.pallas import tpu as pltpu
from jax.sharding import PartitionSpec as P

HD = 64
MESH = pl.DeviceIdType.MESH


def layer_norm(value):
    mean = jnp.mean(value, axis=-1, keepdims=True)
    centered = value - mean
    var = jnp.mean(centered * centered, axis=-1, keepdims=True)
    return centered / jnp.sqrt(var + 1e-07)


def add_rows(left, piece):
    return jnp.dot(left, piece, preferred_element_type=jnp.float32)


def gather_kernel(n, nm, count, *refs):
    hid, wp, codes, rel = refs[:4]
    ins = refs[4 : 4 + count]
    hid_out, wp_out, codes_out, rel_out = refs[4 + count : 8 + count]
    outs = refs[8 + count : 8 + 2 * count]
    (
        local_sem,
        mp_send,
        mp_recv,
        code_send,
        code_recv,
        fwd_send,
        fwd_recv,
        send_sem,
        recv_sem,
    ) = refs[8 + 2 * count :]
    dp, mp = lax.axis_index("dp"), lax.axis_index("mp")
    half = n // 2
    row, col = dp // 2, dp % 2
    pos = row + col * (n - 1 - 2 * row)
    part = rel.shape[2] // nm
    share = pl.ds(pl.multiple_of(mp * part, part), part)

    def at(p):
        p = (p + 2 * n) % n
        h = p // half
        return 2 * (p + h * (n - 1 - 2 * p)) + h

    right, left = at(pos + 1), at(pos - 1)
    barrier = pltpu.get_barrier_semaphore()
    for k in range(1, n):
        pl.semaphore_signal(
            barrier, inc=1, device_id=((dp + k) % n, mp), device_id_type=MESH
        )
    for k in range(1, nm):
        pl.semaphore_signal(
            barrier, inc=1, device_id=(dp, (mp + k) % nm), device_id_type=MESH
        )
    pl.semaphore_wait(barrier, n - 1 + nm - 1)

    pending = {}
    forwards = []

    def send(step, i, way):
        owner = at(pos - step) if way == 0 else at(pos + step)
        if i == 0:
            dst = rel_out.at[owner, way, :, share]
            src = rel.at[way, :, share] if step == 0 else dst
        elif i == 1:
            dst = wp_out.at[owner, mp, way]
            src = wp.at[way] if step == 0 else dst
        else:
            dst = outs[i - 2].at[owner, way]
            src = ins[i - 2].at[way] if step == 0 else dst
        copy = pltpu.make_async_remote_copy(
            src_ref=src,
            dst_ref=dst,
            send_sem=send_sem.at[step, i, way],
            recv_sem=recv_sem.at[step, i, way],
            device_id=(right if way == 0 else left, mp),
            device_id_type=MESH,
        )
        copy.start()
        pending[step, i, way] = copy

    def forward(step, i, way):
        owner = at(pos - step) if way == 0 else at(pos + step)
        piece = rel_out.at[owner, way, :, share] if i == 0 else wp_out.at[owner, mp, way]
        for k in range(1, nm):
            copy = pltpu.make_async_remote_copy(
                src_ref=piece,
                dst_ref=piece,
                send_sem=fwd_send.at[step - 1, i, way, k - 1],
                recv_sem=fwd_recv.at[step - 1, i, way, k - 1],
                device_id=(dp, (mp + k) % nm),
                device_id_type=MESH,
            )
            copy.start()
            forwards.append(copy)

    local = [
        pltpu.make_async_copy(wp, wp_out.at[dp, mp], local_sem.at[0]),
        pltpu.make_async_copy(hid, hid_out.at[mp], local_sem.at[1]),
        pltpu.make_async_copy(codes.at[dp], codes_out.at[dp], local_sem.at[2]),
        pltpu.make_async_copy(rel, rel_out.at[dp], local_sem.at[3]),
    ]
    for i in range(count):
        local.append(pltpu.make_async_copy(ins[i], outs[i].at[dp], local_sem.at[4 + i]))
    others = []

    def start_others():
        for which, (src, dst) in enumerate(((wp, wp_out.at[dp, mp]), (hid, hid_out.at[mp]))):
            for k in range(1, nm):
                others.append(
                    pltpu.make_async_remote_copy(
                        src_ref=src,
                        dst_ref=dst,
                        send_sem=mp_send.at[which, k - 1],
                        recv_sem=mp_recv.at[which, k - 1],
                        device_id=(dp, (mp + k) % nm),
                        device_id_type=MESH,
                    )
                )
        for k in range(1, n):
            others.append(
                pltpu.make_async_remote_copy(
                    src_ref=codes.at[(dp + k) % n],
                    dst_ref=codes_out.at[dp],
                    send_sem=code_send.at[k - 1],
                    recv_sem=code_recv.at[k - 1],
                    device_id=((dp + k) % n, mp),
                    device_id_type=MESH,
                )
            )
        for c in others + local:
            c.start()

    for step in range(n - 1):
        for i in range(count + 2):
            for way in range(2):
                if step:
                    pending[step - 1, i, way].wait_recv()
                send(step, i, way)
                if step and i < 2:
                    forward(step, i, way)
        if step == 0:
            start_others()
    for i in range(count + 2):
        for way in range(2):
            pending[n - 2, i, way].wait_recv()
            if i < 2:
                forward(n - 1, i, way)
    for c in others:
        c.wait()
    for c in local:
        c.wait()
    for c in forwards:
        c.wait()
    for copy in pending.values():
        copy.wait_send()


def gather_all(n, nm, hidden, w_proj, codes, rel, arrays):
    def halves(a):
        return a.reshape((2, a.shape[0] // 2) + a.shape[1:])

    w_proj, rel = halves(w_proj), halves(rel)
    arrays = [halves(a) for a in arrays]
    count = len(arrays)
    bf = jnp.bfloat16
    dma = pltpu.SemaphoreType.DMA
    shapes = [
        jax.ShapeDtypeStruct((nm,) + hidden.shape, bf),
        jax.ShapeDtypeStruct((n, nm) + w_proj.shape, bf),
        jax.ShapeDtypeStruct(codes.shape, jnp.int32),
    ] + [jax.ShapeDtypeStruct((n,) + a.shape, bf) for a in [rel] + arrays]
    out = pl.pallas_call(
        functools.partial(gather_kernel, n, nm, count),
        out_shape=shapes,
        in_specs=[pl.BlockSpec(memory_space=pl.ANY)] * (count + 4),
        out_specs=[pl.BlockSpec(memory_space=pl.ANY)] * (count + 4),
        scratch_shapes=[
            dma((count + 4,)),
            dma((2, nm - 1)),
            dma((2, nm - 1)),
            dma((n - 1,)),
            dma((n - 1,)),
            dma((n - 1, 2, 2, nm - 1)),
            dma((n - 1, 2, 2, nm - 1)),
            dma((n - 1, count + 2, 2)),
            dma((n - 1, count + 2, 2)),
        ],
        compiler_params=pltpu.CompilerParams(collective_id=0, has_side_effects=True),
    )(hidden, w_proj, codes, rel, *arrays)
    flat = [o.reshape((n, o.shape[1] * o.shape[2]) + o.shape[3:]) for o in out[3:]]
    return out[0], out[1], out[2], flat


def layer_kernel(n, nm, *refs):
    (ctx, hid, wo_in, wu_in, wd_in, wp_in, pages_in, where, lens, vec_out, back_out) = refs[:11]
    (wo, wu, wd, wp, pages, load_sem, send_a, recv_a, mid_all, send_d, recv_d) = refs[11:22]
    (seen, found, back, sem_s, sem_r, vec_s, vec_r, back_s, back_r, ring_s, ring_r) = refs[22:]
    dp, mp = lax.axis_index("dp"), lax.axis_index("mp")
    rows, width = hid.shape
    cap, ptok = back.shape[1], pages.shape[1]
    block = wo.shape[2]
    step_cols = max(256, block)
    per = step_cols // block
    chunks = width // step_cols
    loads = [
        pltpu.make_async_copy(src, dst, load_sem.at[i])
        for i, (src, dst) in enumerate(
            ((wo_in, wo), (wu_in, wu), (wd_in, wd.at[dp]), (wp_in, wp), (pages_in, pages))
        )
    ]
    for c in loads:
        c.start()
    barrier = pltpu.get_barrier_semaphore()
    for k in range(1, n):
        pl.semaphore_signal(
            barrier, inc=1, device_id=((dp + k) % n, mp), device_id_type=MESH
        )
    for k in range(1, nm):
        pl.semaphore_signal(
            barrier, inc=1, device_id=(dp, (mp + k) % nm), device_id_type=MESH
        )
    pl.semaphore_wait(barrier, n - 1 + nm - 1)

    half = n // 2
    row, col = dp // 2, dp % 2
    pos = row + col * (n - 1 - 2 * row)

    def at(p):
        p = (p + 2 * n) % n
        h = p // half
        return 2 * (p + h * (n - 1 - 2 * p)) + h

    right, left = at(pos + 1), at(pos - 1)
    ring = []

    def advance(upto):
        for step in range(len(ring), min(upto, n - 2) + 1):
            copies = []
            for way in range(2):
                if step:
                    ring[step - 1][way].wait_recv()
                owner = at(pos - step) if way == 0 else at(pos + step)
                dst = wd.at[owner, way]
                copy = pltpu.make_async_remote_copy(
                    src_ref=dst if step else wd_in.at[way],
                    dst_ref=dst,
                    send_sem=ring_s.at[step, way],
                    recv_sem=ring_r.at[step, way],
                    device_id=(right if way == 0 else left, mp),
                    device_id_type=MESH,
                )
                copy.start()
                copies.append(copy)
            ring.append(copies)

    advance(0)

    def piece(w, j):
        parts = [w[j * per + t].reshape(-1, block) for t in range(per)]
        return parts[0] if per == 1 else jnp.concatenate(parts, axis=1)

    def mp_copy(stage, k, j, src, dst):
        return pltpu.make_async_remote_copy(
            src_ref=src,
            dst_ref=dst,
            send_sem=sem_s.at[stage, k - 1, j],
            recv_sem=sem_r.at[stage, k - 1, j],
            device_id=(dp, (mp + k) % nm),
            device_id_type=MESH,
        )

    order = [k for k in range(1, nm) if k != 1] + [1]
    started = []

    loads[0].wait()
    own = []
    for j in range(chunks):
        weight = piece(wo, j)
        for k in order:
            block_rows = ctx[pl.ds(pl.multiple_of((mp + k) % nm * rows, rows), rows), :]
            send_a[k - 1, j] = add_rows(block_rows, weight).astype(jnp.bfloat16)
            copy = mp_copy(0, k, j, send_a.at[k - 1, j], recv_a.at[k - 1, j])
            copy.start()
            started.append(copy)
        own.append(add_rows(ctx[pl.ds(pl.multiple_of(mp * rows, rows), rows), :], weight))
    advance(1)
    sums = []
    for j in range(chunks):
        total = own[j]
        for k in range(1, nm):
            mp_copy(0, k, j, send_a.at[k - 1, j], recv_a.at[k - 1, j]).wait_recv()
            total = total + recv_a[k - 1, j].astype(jnp.float32)
        sums.append(total)
    advance(2)
    attn = jnp.concatenate(sums, axis=1)
    mid = layer_norm(hid[...].astype(jnp.float32) + attn).astype(jnp.bfloat16)
    mid_all[mp] = mid
    for k in order:
        copy = mp_copy(1, k, 0, mid_all.at[mp], mid_all.at[mp])
        copy.start()
        started.append(copy)
    advance(3)
    loads[1].wait()
    loads[2].wait()
    for k in range(1, nm):
        mp_copy(1, k, 0, mid_all.at[mp], mid_all.at[mp]).wait_recv()
    advance(4)
    group_mid = mid_all[...].reshape(nm * rows, width)
    inner = []
    hidden_cols = wu.shape[1]
    for j in range(hidden_cols // 256):
        up = add_rows(group_mid, wu[:, j * 256 : (j + 1) * 256])
        act = 0.5 * up * (1.0 + lax.erf(up * (0.5**0.5)))
        inner.append(act.astype(jnp.bfloat16))
        if j % 2 == 0:
            advance(5 + j // 2)
    advance(n - 2)
    for copy in ring[n - 2]:
        copy.wait_recv()
    inner = jnp.concatenate(inner, axis=1)
    for j in range(chunks):
        down = add_rows(inner, piece(wd, j)).astype(jnp.bfloat16)
        send_d[j] = down.reshape(nm, rows, step_cols)
        for k in order:
            copy = mp_copy(2, k, j, send_d.at[j, (mp + k) % nm], recv_d.at[k - 1, j])
            copy.start()
            started.append(copy)
    sums = []
    for j in range(chunks):
        total = send_d[j, mp].astype(jnp.float32)
        for k in range(1, nm):
            mp_copy(2, k, j, send_d.at[j, mp], recv_d.at[k - 1, j]).wait_recv()
            total = total + recv_d[k - 1, j].astype(jnp.float32)
        sums.append(total)
    mlp = jnp.concatenate(sums, axis=1)
    state = layer_norm(mid_all[mp].astype(jnp.float32) + mlp).astype(jnp.bfloat16)
    loads[3].wait()
    proj = add_rows(state, wp[...])
    norm = jnp.sqrt(jnp.sum(proj * proj, axis=-1, keepdims=True) + 1e-06)
    vectors = (proj / norm).astype(jnp.bfloat16)
    vec_out[...] = vectors
    seen[dp] = vectors

    def vec_copy(k):
        return pltpu.make_async_remote_copy(
            src_ref=seen.at[dp],
            dst_ref=seen.at[dp],
            send_sem=vec_s.at[k - 1],
            recv_sem=vec_r.at[k - 1],
            device_id=((dp + k) % n, mp),
            device_id_type=MESH,
        )

    def back_copy(k):
        return pltpu.make_async_remote_copy(
            src_ref=found.at[k - 1],
            dst_ref=back.at[dp],
            send_sem=back_s.at[k - 1],
            recv_sem=back_r.at[k - 1],
            device_id=((dp - k + n) % n, mp),
            device_id_type=MESH,
        )

    for k in range(1, n):
        vec_copy(k).start()
    loads[4].wait()
    token = lax.broadcasted_iota(jnp.int32, (ptok, rows), 0)

    def match(source):
        vec = seen[source]
        best = []
        for g in range(0, cap, 8):
            slots = [where[source * cap + g + r] for r in range(8)]
            chunk = jnp.concatenate([pages[slot] for slot in slots], axis=0)
            sim = lax.dot_general(
                chunk, vec, (((1,), (1,)), ((), ())), preferred_element_type=jnp.float32
            )
            for r in range(8):
                part = sim[r * ptok : (r + 1) * ptok]
                part = jnp.where(token < lens[slots[r]], part, -1e30)
                best.append(jnp.max(part, axis=0, keepdims=True))
        return jnp.concatenate(best, axis=0).astype(jnp.bfloat16)

    back[dp] = match(dp)

    def work(k, carry):
        vec_copy(k).wait_recv()
        found[k - 1] = match((dp - k + n) % n)
        back_copy(k).start()
        return carry

    lax.fori_loop(1, n, work, 0)
    for k in range(1, n):
        back_copy(k).wait_recv()
    back_out[...] = back[...]
    for k in range(1, n):
        vec_copy(k).wait_send()
        back_copy(k).wait_send()
    for c in started:
        c.wait_send()
    for copies in ring:
        for c in copies:
            c.wait_send()


def layer_and_score(n, nm, cap, ctx, hid, wo, wu, wd, wp, pages, where, lens):
    rows, width = hid.shape
    block = wo.shape[2]
    step_cols = max(256, block)
    chunks = width // step_cols
    bf = jnp.bfloat16
    vmem = pl.BlockSpec(memory_space=pltpu.VMEM)
    smem = pl.BlockSpec(memory_space=pltpu.SMEM)
    far = pl.BlockSpec(memory_space=pl.ANY)
    dma = pltpu.SemaphoreType.DMA
    wd = wd.reshape((2, wd.shape[0] // 2) + wd.shape[1:])
    shapes = [wo.shape, wu.shape, (n,) + wd.shape, wp.shape, pages.shape]
    scratch = [pltpu.VMEM(shape, bf) for shape in shapes] + [
        dma((5,)),
        pltpu.VMEM((nm - 1, chunks, rows, step_cols), bf),
        pltpu.VMEM((nm - 1, chunks, rows, step_cols), bf),
        pltpu.VMEM((nm, rows, width), bf),
        pltpu.VMEM((chunks, nm, rows, step_cols), bf),
        pltpu.VMEM((nm - 1, chunks, rows, step_cols), bf),
        pltpu.VMEM((n, rows, wp.shape[1]), bf),
        pltpu.VMEM((n - 1, cap, rows), bf),
        pltpu.VMEM((n, cap, rows), bf),
        dma((3, nm - 1, chunks)),
        dma((3, nm - 1, chunks)),
        dma((n - 1,)),
        dma((n - 1,)),
        dma((n - 1,)),
        dma((n - 1,)),
        dma((n - 1, 2)),
        dma((n - 1, 2)),
    ]
    return pl.pallas_call(
        functools.partial(layer_kernel, n, nm),
        out_shape=[
            jax.ShapeDtypeStruct((rows, wp.shape[1]), bf),
            jax.ShapeDtypeStruct((n, cap, rows), bf),
        ],
        in_specs=[vmem, vmem, far, far, far, far, far, smem, smem],
        out_specs=[vmem, vmem],
        scratch_shapes=scratch,
        compiler_params=pltpu.CompilerParams(
            collective_id=1, has_side_effects=True, vmem_limit_bytes=60 * 2**20
        ),
    )(ctx, hid, wo, wu, wd, wp, pages, where, lens)


def body(
    hidden,
    query_weight,
    w_key,
    w_value,
    rel_table,
    rel_bucket,
    w_out,
    w_up,
    w_down,
    w_proj,
    pages,
    page_len,
    slot_per_page,
    candidates,
):
    n, nm = lax.axis_size("dp"), lax.axis_size("mp")
    qry_dev, qlen, width = hidden.shape
    heads_local = query_weight.shape[1] // HD
    cols = query_weight.shape[1]

    pg_dev = pages.shape[0]
    ncand, ppc = (candidates.shape[1], candidates.shape[2])
    req = qry_dev * ncand * ppc
    cap = 2 * req // n
    slots = slot_per_page[candidates.reshape(req)]
    dest = slots // pg_dev
    order = jnp.arange(req, dtype=jnp.int32)
    earlier = (dest[:, None] == dest[None, :]) & (order[None, :] < order[:, None])
    place = jnp.sum(earlier.astype(jnp.int32), axis=1)
    index = dest * cap + place
    codes = jnp.zeros((n * cap,), jnp.int32).at[index].set(slots % pg_dev)
    tokens, proj_w, where_local, (rel, wq, wk, wv, wo, wu) = gather_all(
        n,
        nm,
        hidden.reshape(qry_dev * qlen, width),
        w_proj,
        codes.reshape(n, 1, cap),
        rel_table,
        (query_weight, w_key, w_value, w_out, w_up),
    )
    group = nm * qry_dev
    flat = tokens.reshape(group * qlen, width)
    wq, wk, wv = (w.reshape(width, cols) for w in (wq, wk, wv))
    rel = rel.reshape(-1, width)
    wu = wu.reshape(width, -1)
    qsum = add_rows(flat, wq)
    ksum = add_rows(flat, wk)
    vsum = add_rows(flat, wv)
    rel_q = add_rows(rel, wq).astype(jnp.bfloat16)
    rel_k = add_rows(rel, wk).astype(jnp.bfloat16)
    nbuck = rel_q.shape[0]
    qx = qsum.astype(jnp.bfloat16).reshape(group, qlen, heads_local, HD)
    kx = ksum.astype(jnp.bfloat16).reshape(group, qlen, heads_local, HD)
    vx = vsum.astype(jnp.bfloat16).reshape(group, qlen, heads_local, HD)
    rel_q = rel_q.reshape(nbuck, heads_local, HD)
    rel_k = rel_k.reshape(nbuck, heads_local, HD)
    onehot = (rel_bucket[:, :, None] == jnp.arange(nbuck, dtype=jnp.int32)[None, None, :]).astype(
        jnp.float32
    )
    scale = 1.0 / jnp.sqrt(jnp.float32(3 * HD))
    content = jnp.einsum("qihd,qjhd->qhij", qx, kx, preferred_element_type=jnp.float32)
    along_axis_name = jnp.einsum("qihd,bhd->qhib", qx, rel_k, preferred_element_type=jnp.float32)
    c2p = jnp.einsum("qhib,ijb->qhij", along_axis_name, onehot, precision=lax.Precision.HIGHEST)
    back = jnp.einsum("qjhd,bhd->qhjb", kx, rel_q, preferred_element_type=jnp.float32)
    p2c = jnp.einsum("qhjb,jib->qhij", back, onehot, precision=lax.Precision.HIGHEST)
    logits = (content + c2p + p2c) * scale
    probs = jax.nn.softmax(logits, axis=-1).astype(jnp.bfloat16)
    context_rows = jnp.einsum("qhij,qjhd->qihd", probs, vx, preferred_element_type=jnp.float32)
    context_rows = context_rows.astype(jnp.bfloat16).reshape(group * qlen, cols)
    width_out = w_proj.shape[1]
    vectors, back_home = layer_and_score(
        n,
        nm,
        cap,
        context_rows,
        hidden.reshape(qry_dev * qlen, width),
        wo,
        wu,
        w_down,
        proj_w.reshape(width, width_out),
        pages,
        where_local.reshape(-1),
        page_len,
    )
    best = back_home.reshape(n * cap, qry_dev * qlen)[index].astype(jnp.float32)
    best = best.reshape(qry_dev, ncand, ppc, qry_dev, qlen)
    best = jnp.stack([best[q, :, :, q] for q in range(qry_dev)])
    scores = jnp.sum(jnp.max(best, axis=2), axis=-1)
    return (vectors.reshape(qry_dev, qlen, width_out), scores)


def solution(mesh):
    in_specs = (
        P(("dp", "mp"), None, None),
        P("dp", "mp"),
        P("dp", "mp"),
        P("dp", "mp"),
        P("dp", None),
        P(),
        P("mp", "dp"),
        P("dp", "mp"),
        P("mp", "dp"),
        P(("dp", "mp"), None),
        P("dp", None, None),
        P("dp"),
        P(),
        P(("dp", "mp"), None, None),
    )
    out_specs = (P(("dp", "mp"), None, None), P(("dp", "mp"), None))
    return jax.shard_map(body, mesh=mesh, in_specs=in_specs, out_specs=out_specs, check_vma=False)
```
